512 devices in a mesh: ex: 32 (over y, x, core), tp: 16 (over z).
Axes of the slice: x: 4, y: 4, z: 16, core: 2. Of those that a mesh axis runs over, the one named last changes fastest.
Arguments:
- activations: bfloat16 [16384, 8192], P('ex', 'tp'), may hold values from -6 to 6
- out_grads: bfloat16 [16384, 29568], P('ex', 'tp'), may hold values from -6 to 6
- basis_in: bfloat16 [8192, 512], P('tp', 'ex'), may hold values from -0.0625 to 0.0625
- basis_out: bfloat16 [29568, 512], P('tp', 'ex'), may hold values from -0.03125 to 0.03125
- eigen: float32 [512, 512], replicated, may hold values from 1 to 10
- lengths: int32 [32], P('ex'), may hold values from 64 to 512, as said below
- query_in: bfloat16 [512, 8192], P(None, 'tp'), may hold values from -0.09375 to 0.09375
- query_out: bfloat16 [512, 8192], P(None, 'tp'), may hold values from -0.09375 to 0.09375
Outputs:
- scores: float32 [32, 1024], P('ex', 'tp')
The draws below stay inside these ranges and needn't reach their ends.
Inputs may be any that keep to these rules, and one draw needn't show every extreme that they name: `lengths`: some sequence has all 512 tokens counted in every draw.
All inputs are finite; a program needn't handle non-finite values.
Results may differ from the reference program's by a relative error of at most 0.0049.
Values may be sent and summed in bfloat16 or wider, within the bound.
No kernel may reach another device: no remote copies, remote signals or barrier semaphores. Data moves between devices by JAX's collectives and lax.ppermute only.
A program may use at most 64 MiB of HBM per device.

```python
import math
import jax
import jax.numpy as jnp
from jax import lax

D = 8192
FF = 29568
LEN = 512
KA = 512
KG = 512
RANK = 8
NQ = 1024
SEQS = 32


def draw_lengths(key, part):
    key = jax.random.fold_in(key, 7)
    first_key, second_key = jax.random.split(key)
    values = jax.random.randint(first_key, (SEQS,), LEN // 8, LEN + 1)
    chosen = jax.random.randint(second_key, (), 0, SEQS)
    return jnp.where(jnp.arange(SEQS) == chosen, LEN, values).astype(jnp.int32)


def shard_levels(stream_key, dims, shards, least, high):
    def one(axis_at, parts):
        draws = jax.random.uniform(jax.random.fold_in(jax.random.fold_in(stream_key, 6), axis_at), (parts,), jnp.float32, least / len(shards), high / len(shards))
        return jnp.repeat(jnp.exp(draws), dims[axis_at] // parts).reshape((-1,) + (1,) * (len(dims) - axis_at - 1))

    gain = one(*shards[0])
    for cut in shards[1:]:
        gain = gain * one(*cut)
    return gain


def gaussian(key, shape, spread, most, cuts=(), kind=jnp.bfloat16):
    values = spread * jax.random.normal(key, shape, jnp.float32)
    if cuts:
        values = values * shard_levels(key, shape, cuts, -0.22, 0.18)
    return jnp.clip(values, -most, most).astype(kind)


def setup_inputs(seed: int = 0) -> dict:
    key_list = jax.random.split(jax.random.key(seed), 9)
    return {
        "activations": gaussian(key_list[0], (SEQS * LEN, D), 1.0, 6.0, ((0, 32), (1, 16))),
        "out_grads": gaussian(key_list[1], (SEQS * LEN, FF), 1.0, 6.0, ((0, 32), (1, 16))),
        "basis_in": gaussian(key_list[2], (D, KA), D ** -0.5, 0.0625, ((0, 16), (1, 32))),
        "basis_out": gaussian(key_list[3], (FF, KG), FF ** -0.5, 0.03125, ((0, 16), (1, 32))),
        "eigen": jnp.clip(jnp.exp(jax.random.uniform(key_list[4], (KA, KG), jnp.float32, math.log(1.0), math.log(10.0))), 1.0, 10.0),
        "lengths": draw_lengths(jax.random.fold_in(key_list[8], 71), 0),
        "query_in": gaussian(key_list[6], (KA, NQ * RANK), (KA * RANK) ** -0.5, 0.09375, ((1, 16),)),
        "query_out": gaussian(key_list[7], (KG, NQ * RANK), (KG * RANK) ** -0.5, 0.09375, ((1, 16),)),
    }


DAMP = 0.1


def reference(activations, out_grads, basis_in, basis_out, eigen, lengths, query_in, query_out):
    rot_in = jnp.dot(activations, basis_in, preferred_element_type=jnp.float32).astype(jnp.bfloat16)
    rot_out = jnp.dot(out_grads, basis_out, preferred_element_type=jnp.float32).astype(jnp.bfloat16)
    rows_in = rot_in.reshape(SEQS, LEN, KA)
    rows_out = rot_out.reshape(SEQS, LEN, KG)
    positions = jnp.arange(LEN, dtype=jnp.int32)
    query_wide = query_in.astype(jnp.float32)

    def per_sequence(items):
        seq_in, seq_out, seq_length = items
        kept_rows = (positions < seq_length).astype(jnp.bfloat16)[:, None]
        kept = seq_out * kept_rows
        statistic = lax.dot_general(seq_in, kept, (((0,), (0,)), ((), ())), preferred_element_type=jnp.float32)
        scaled = (statistic / (eigen + DAMP)).astype(jnp.bfloat16)
        weighted = jnp.dot(scaled, query_out, preferred_element_type=jnp.float32)
        summed = jnp.sum(weighted * query_wide, axis=0)
        return summed.reshape(NQ, RANK).sum(axis=1)

    return lax.map(per_sequence, (rows_in, rows_out, lengths))
```

```python
import jax
import jax.numpy as jnp
from jax import lax
from jax.sharding import Mesh
from jax.sharding import PartitionSpec as P

RANK = 8
DAMP = 0.1
RING = 16
PLANE = ("y", "x")
LINE = ("c", "z")


def shift(x, forward, backward):
    pairs = []
    for core, step in enumerate((forward, backward)):
        for at in range(RING):
            pairs.append((core * RING + at, core * RING + (at + step) % RING))
    return lax.ppermute(x, LINE, pairs)


def whole_basis(columns):
    kept, width = columns.shape
    near = lax.all_to_all(jnp.broadcast_to(columns[None], (16, kept, width)), PLANE, 0, 0)
    far = lax.ppermute(near, "c", [(0, 1), (1, 0)])
    first = lax.axis_index("c") == 0
    both = jnp.stack([jnp.where(first, near, far), jnp.where(first, far, near)], axis=1)
    return both.reshape(-1, width)


def reduce_step(parts, near, far):
    own = parts[0]
    one = shift(parts[1], near, -near)
    two = shift(parts[2], -near, near)
    three = shift(parts[3], far, -far)
    f = jnp.float32
    return own + one.astype(f) + two.astype(f) + three.astype(f)


def shards(activations, out_grads, basis_in, basis_out, eigen, lengths, query_in, query_out):
    f32, bf16, f16 = jnp.float32, jnp.bfloat16, jnp.float16
    at = lax.axis_index("z")
    low, high = at % 4, at // 4
    depth = basis_in.shape[0]
    basis = whole_basis(jnp.concatenate([basis_in.T, basis_out.T], axis=1))
    basis_i, basis_o = basis[:, :depth], basis[:, depth:]

    def rotated(k):
        start = ((low + k + 4) % 4) * 128
        a = lax.dynamic_slice_in_dim(activations, start, 128, 0)
        g = lax.dynamic_slice_in_dim(out_grads, start, 128, 0)
        dims = (((1,), (1,)), ((), ()))
        left = lax.dot_general(a, basis_i, dims, preferred_element_type=f32)
        right = lax.dot_general(g, basis_o, dims, preferred_element_type=f32)
        return jnp.concatenate([left, right], axis=1)

    sign = 1 - 2 * lax.axis_index("c")
    turns = (0, sign, -sign, 2)
    rows = [rotated(k) for k in turns]
    mine = reduce_step([rows[0]] + [r.astype(f16) for r in rows[1:]], 1, 2)
    quarter = [lax.dynamic_slice_in_dim(mine, ((high + k + 4) % 4) * 32, 32, 0) for k in turns]
    mine = reduce_step([quarter[0]] + [r.astype(f16) for r in quarter[1:]], 4, 8)

    position = low * 128 + high * 32 + lax.broadcasted_iota(jnp.int32, (32, 1), 0)
    counted = (position < lengths[0]).astype(bf16)
    half = mine.shape[1] // 2
    mine = mine.astype(bf16)
    mine = jnp.concatenate([mine[:, :half], mine[:, half:] * counted], axis=1)
    held = jnp.concatenate([mine, shift(mine, 4, -4), shift(mine, -4, 4), shift(mine, 8, -8)], axis=0)
    pieces = [held, shift(held, 1, -1), shift(held, -1, 1), shift(held, 2, -2)]
    statistic = 0.0
    for piece in pieces:
        statistic += lax.dot_general(
            piece[:, :half], piece[:, half:], (((0,), (0,)), ((), ())), preferred_element_type=f32
        )
    scaled = (statistic / (eigen + DAMP)).astype(bf16)
    weighted = jnp.dot(scaled, query_out, preferred_element_type=f32)
    summed = jnp.sum(weighted * query_in.astype(f32), axis=0)
    return summed.reshape(-1, RANK).sum(axis=1)[None, :]


def solution(mesh):
    fine = Mesh(mesh.devices.reshape(4, 4, 2, RING), ("y", "x", "c", "z"))
    ex = ("y", "x", "c")
    in_specs = (P(ex, "z"), P(ex, "z"), P("z", ex), P("z", ex), P(), P(ex), P(None, "z"), P(None, "z"))
    return jax.shard_map(shards, mesh=fine, in_specs=in_specs, out_specs=P(ex, "z"), check_vma=False)
```

```python
import jax
import jax.numpy as jnp
from jax import lax
from jax.sharding import Mesh
from jax.sharding import PartitionSpec as P

RANK = 8
DAMP = 0.1
UP_IN = 16.0
UP_OUT = 8.0
LIFT_IN = 2.0**19
LIFT_OUT = 2.0**20


def rotate(rows, columns):
    return lax.dot_general(rows, columns, (((1,), (1,)), ((), ())), preferred_element_type=jnp.float32)


def shards(activations, out_grads, basis_in, basis_out, eigen, lengths, query_in, query_out):
    f32, bf16, f16 = jnp.float32, jnp.bfloat16, jnp.float16
    depth = basis_in.shape[0]
    lifted = [basis_in.T.astype(f32) * LIFT_IN, basis_out.T.astype(f32) * LIFT_OUT]
    own = jnp.concatenate(lifted, axis=1).astype(f16)
    basis = lax.all_gather(own, ("y", "x", "c"), axis=0, tiled=True).astype(bf16)
    low_in, low_out = UP_IN / LIFT_IN, UP_OUT / LIFT_OUT
    left = rotate(activations, basis[:, :depth]) * low_in
    right = rotate(out_grads, basis[:, depth:]) * low_out
    partial = jnp.concatenate([left.astype(f16), right.astype(f16)], axis=1)
    rotated = lax.psum(partial, "z").astype(f32)
    half = rotated.shape[1] // 2
    position = lax.broadcasted_iota(jnp.int32, (rotated.shape[0], 1), 0)
    counted = (position < lengths[0]).astype(f32)
    inputs = (rotated[:, :half] * (1 / UP_IN)).astype(bf16)
    outputs = (rotated[:, half:] * (counted * (1 / UP_OUT))).astype(bf16)
    statistic = lax.dot_general(inputs, outputs, (((0,), (0,)), ((), ())), preferred_element_type=f32)
    scaled = (statistic / (eigen + DAMP)).astype(bf16)
    weighted = jnp.dot(scaled, query_out, preferred_element_type=f32)
    summed = jnp.sum(weighted * query_in.astype(f32), axis=0)
    return summed.reshape(-1, RANK).sum(axis=1)[None, :]


def solution(mesh):
    fine = Mesh(mesh.devices.reshape(4, 4, 2, 16), ("y", "x", "c", "z"))
    ex = ("y", "x", "c")
    in_specs = (P(ex, "z"), P(ex, "z"), P("z", ex), P("z", ex), P(), P(ex), P(None, "z"), P(None, "z"))
    return jax.shard_map(shards, mesh=fine, in_specs=in_specs, out_specs=P(ex, "z"), check_vma=False)
```

```python
import jax
import jax.numpy as jnp
from jax import lax
from jax.sharding import Mesh
from jax.sharding import PartitionSpec as P

RANK = 8
DAMP = 0.1
UP_IN = 16.0
UP_OUT = 8.0
LIFT = 2.0**19


def rotate(rows, columns):
    return lax.dot_general(rows, columns, (((1,), (1,)), ((), ())), preferred_element_type=jnp.float32)


def shards(activations, out_grads, basis_in, basis_out, eigen, lengths, query_in, query_out):
    f32, bf16, f16 = jnp.float32, jnp.bfloat16, jnp.float16
    depth = basis_in.shape[0]
    own = jnp.concatenate([basis_in.T, basis_out.T], axis=1)
    own = (own.astype(f32) * LIFT).astype(f16)
    basis = lax.all_gather(own, ("y", "x", "c"), axis=0, tiled=True).astype(bf16)
    right = (rotate(out_grads, basis[:, depth:]) * (UP_OUT / LIFT)).astype(f16)
    basis, right = lax.optimization_barrier((basis, right))
    left = (rotate(activations, basis[:, :depth]) * (UP_IN / LIFT)).astype(f16)
    left, right = lax.psum((left, right), "z")
    position = lax.broadcasted_iota(jnp.int32, (right.shape[0], 1), 0)
    counted = (position < lengths[0]).astype(f32)
    inputs = (left.astype(f32) * (1 / UP_IN)).astype(bf16)
    outputs = (right.astype(f32) * (counted * (1 / UP_OUT))).astype(bf16)
    statistic = lax.dot_general(inputs, outputs, (((0,), (0,)), ((), ())), preferred_element_type=f32)
    scaled = (statistic / (eigen + DAMP)).astype(bf16)
    weighted = jnp.dot(scaled, query_out, preferred_element_type=f32)
    summed = jnp.sum(weighted * query_in.astype(f32), axis=0)
    return summed.reshape(-1, RANK).sum(axis=1)[None, :]


def solution(mesh):
    fine = Mesh(mesh.devices.reshape(4, 4, 2, 16), ("y", "x", "c", "z"))
    ex = ("y", "x", "c")
    in_specs = (P(ex, "z"), P(ex, "z"), P("z", ex), P("z", ex), P(), P(ex), P(None, "z"), P(None, "z"))
    return jax.shard_map(shards, mesh=fine, in_specs=in_specs, out_specs=P(ex, "z"), check_vma=False)
```

```python
import jax
import jax.numpy as jnp
from jax import lax
from jax.sharding import Mesh
from jax.sharding import PartitionSpec as P

RANK = 8
DAMP = 0.1
UP_IN = 16.0
UP_OUT = 8.0
LIFT = 2.0**19


def rotate(rows, columns):
    return lax.dot_general(rows, columns, (((1,), (1,)), ((), ())), preferred_element_type=jnp.float32)


def shards(activations, out_grads, basis_in, basis_out, eigen, lengths, query_in, query_out):
    f32, bf16, f16 = jnp.float32, jnp.bfloat16, jnp.float16
    depth = basis_in.shape[0]
    own = jnp.concatenate([basis_in.T, basis_out.T], axis=1)
    own = (own.astype(f32) * LIFT).astype(f16)
    basis = lax.all_gather(own, ("y", "x", "c"), axis=0, tiled=True)
    right = (rotate(out_grads, basis[:, depth:].astype(bf16)) * (UP_OUT / LIFT)).astype(f16)
    basis, right = lax.optimization_barrier((basis, right))
    left = (rotate(activations, basis[:, :depth].astype(bf16)) * (UP_IN / LIFT)).astype(f16)
    left, right = lax.psum((left, right), "z")
    position = lax.broadcasted_iota(jnp.int32, (right.shape[0], 1), 0)
    counted = (position < lengths[0]).astype(f32)
    inputs = (left.astype(f32) * (1 / UP_IN)).astype(bf16)
    outputs = (right.astype(f32) * (counted * (1 / UP_OUT))).astype(bf16)
    statistic = lax.dot_general(inputs, outputs, (((0,), (0,)), ((), ())), preferred_element_type=f32)
    scaled = (statistic / (eigen + DAMP)).astype(bf16)
    weighted = jnp.dot(scaled, query_out, preferred_element_type=f32)
    summed = jnp.sum(weighted * query_in.astype(f32), axis=0)
    return summed.reshape(-1, RANK).sum(axis=1)[None, :]


def solution(mesh):
    fine = Mesh(mesh.devices.reshape(4, 4, 2, 16), ("y", "x", "c", "z"))
    ex = ("y", "x", "c")
    in_specs = (P(ex, "z"), P(ex, "z"), P("z", ex), P("z", ex), P(), P(ex), P(None, "z"), P(None, "z"))
    return jax.shard_map(shards, mesh=fine, in_specs=in_specs, out_specs=P(ex, "z"), check_vma=False)
```
